256 devices in a mesh: ctx: 32 (over z, y_lo, core), fsdp: 8 (over y_hi, x).
Axes of the slice: x: 4, y: 4 (y_hi: 2, y_lo: 2; y = y_hi * 2 + y_lo), z: 8, core: 2. Of those that a mesh axis runs over, the one named last changes fastest.
Arguments:
- hidden: bfloat16 [4096, 7168], P('ctx', 'fsdp'), may hold values from -6 to 6
- block_kind: int32 [32, 32], P('ctx'), may hold values from 0 to 2, as said below
- policy_queries: bfloat16 [4096, 12288], P('ctx', 'fsdp'), may hold values from -64 to 64
- policy_down: bfloat16 [7168, 576], P('fsdp'), may hold values from -0.0625 to 0.0625
- policy_gain: float32 [512], replicated, may hold values from 0.1 to 1.9
- policy_up: bfloat16 [64, 512, 256], P('fsdp', 'ctx'), may hold values from -0.5 to 0.5
- frozen_queries: bfloat16 [4096, 12288], P('ctx', 'fsdp'), may hold values from -64 to 64
- frozen_down: bfloat16 [7168, 576], P('fsdp'), may hold values from -0.0625 to 0.0625
- frozen_gain: float32 [512], replicated, may hold values from 0.1 to 1.9
- frozen_up: bfloat16 [64, 512, 256], P('fsdp', 'ctx'), may hold values from -0.5 to 0.5
Outputs:
- policy_out: bfloat16 [4096, 8192], P('ctx', 'fsdp')
- frozen_out: bfloat16 [4096, 8192], P('ctx', 'fsdp')
The draws below stay inside these ranges and needn't reach their ends.
Inputs may be any that keep to these rules, and one draw needn't show every extreme that they name: block_kind[i, j] rules query block i and key block j: 0 nothing visible, 1 all visible, 2 keys at or before the query; the diagonal is 2, no other entry is 2, and nothing above the diagonal is visible.
All inputs are finite; a program needn't handle non-finite values.
Results may differ from the reference program's by a relative error of at most 0.009.
The reference program's roundings to bfloat16 on the way count: a program that leaves them out, or rounds other values in their place, can miss the bound.
Values may be sent and summed in bfloat16 or wider, within the bound.
No kernel may reach another device: no remote copies, remote signals or barrier semaphores. Data moves between devices by JAX's collectives and lax.ppermute only.
A program may use at most 128 MiB of HBM per device.

```python
import jax
import jax.numpy as jnp
from jax import lax

D = 7168
H = 64
QN = 128
QR = 64
L = 512
VD = 128
BLOCK = 128
TOKENS = 4096
NB = 32


def scaled_normal(key, row_top, clip_level):
    scale_key, value_key = jax.random.split(key)
    exponents = jax.random.uniform(scale_key, (TOKENS, H, 1), minval=0.0, maxval=1.0)
    row_scale = row_top ** exponents
    values = jax.random.normal(value_key, (TOKENS, H, QN + QR), dtype=jnp.float32) * 1.5 * row_scale
    return jnp.clip(values, -clip_level, clip_level).reshape(TOKENS, H * (QN + QR))


def draw_policy_queries(key, part):
    key = jax.random.fold_in(key, 7)
    return scaled_normal(key, 1.0, 8.0).astype(jnp.bfloat16)


def draw_frozen_queries(key, part):
    key = jax.random.fold_in(key, 9)
    return scaled_normal(key, 1.0, 8.0).astype(jnp.bfloat16)


def draw_block_kind(key, part):
    key = jax.random.fold_in(key, 13)
    block_count = TOKENS // BLOCK
    answer_cuts = max(3, min(15, block_count // 4))
    prompt_key, order_key = jax.random.split(key)
    prompt_blocks = jax.random.randint(prompt_key, (), max(2, block_count // 8), block_count // 2 + 1)
    block_index = jnp.arange(block_count, dtype=jnp.int32)
    block_order = jax.random.permutation(order_key, block_count)
    candidate = block_index > prompt_blocks
    smaller = jnp.sum((candidate[None, :] & (block_order[None, :] < block_order[:, None])).astype(jnp.int32), axis=1)
    starts = (block_index == prompt_blocks) | candidate & (smaller < answer_cuts)
    segment = jnp.cumsum(starts.astype(jnp.int32))
    earlier = block_index[None, :] < block_index[:, None]
    shared = (segment[None, :] == 0) | (segment[None, :] == segment[:, None])
    kind_table = jnp.where(block_index[None, :] == block_index[:, None], 2, jnp.where(earlier & shared, 1, 0))
    return kind_table.astype(jnp.int32)


def shard_levels(key, dims, cuts, smallest, high):
    def one(dim, shards_of):
        steps = jax.random.uniform(jax.random.fold_in(jax.random.fold_in(key, 6), dim), (shards_of,), jnp.float32, smallest / len(cuts), high / len(cuts))
        return jnp.repeat(jnp.exp(steps), dims[dim] // shards_of).reshape((-1,) + (1,) * (len(dims) - dim - 1))

    loudness = one(*cuts[0])
    for cut in cuts[1:]:
        loudness = loudness * one(*cut)
    return loudness


def scatter_about(rng, shape, spread, bound, pieces=(), held_as=jnp.bfloat16):
    level = shard_levels(rng, shape, pieces, -0.22, 0.18) if pieces else 1.0
    result = jax.random.normal(rng, shape, jnp.float32) * spread * level
    return jnp.minimum(jnp.maximum(result, -bound), bound).astype(held_as)


def setup_inputs(seed: int = 0) -> dict:
    key_list = jax.random.split(jax.random.key(seed), 11)
    hidden = scatter_about(key_list[0], (TOKENS, D), 1.0, 6.0, ((0, 32), (1, 8)))
    block_kind = draw_block_kind(jax.random.fold_in(key_list[10], 71), 0)
    policy_queries = draw_policy_queries(jax.random.fold_in(key_list[10], 71), 0)
    policy_down = scatter_about(key_list[3], (D, L + QR), D ** -0.5, 0.0625, ((0, 8),))
    policy_gain = jnp.clip(1.0 + 0.18 * jax.random.normal(key_list[4], (L,), jnp.float32), 0.1, 1.9)
    policy_up = scatter_about(key_list[5], (H, L, QN + VD), QN ** -0.5, 0.5, ((0, 8), (1, 32)))
    frozen_queries = draw_frozen_queries(jax.random.fold_in(key_list[10], 71), 0)
    frozen_down = scatter_about(key_list[7], (D, L + QR), D ** -0.5, 0.0625, ((0, 8),))
    frozen_gain = jnp.clip(1.0 + 0.18 * jax.random.normal(key_list[8], (L,), jnp.float32), 0.1, 1.9)
    frozen_up = scatter_about(key_list[9], (H, L, QN + VD), QN ** -0.5, 0.5, ((0, 8), (1, 32)))
    return {"hidden": hidden, "block_kind": block_kind, "policy_queries": policy_queries, "policy_down": policy_down, "policy_gain": policy_gain, "policy_up": policy_up, "frozen_queries": frozen_queries, "frozen_down": frozen_down, "frozen_gain": frozen_gain, "frozen_up": frozen_up}


norm_eps = 1e-06
rope_base = 10000.0

def rotate(values, positions):
    half_width = values.shape[1] // 2
    frequency = rope_base ** (-2.0 * jnp.arange(half_width, dtype=jnp.float32) / values.shape[1])
    angles = positions[:, None] * frequency[None, :]
    cosine = jnp.cos(angles)
    sine_term = jnp.sin(angles)
    first_half = values[:, :half_width]
    second_half = values[:, half_width:]
    return jnp.concatenate([first_half * cosine - second_half * sine_term, second_half * cosine + first_half * sine_term], axis=1)

def finish_keys(raw_sums, gain, positions):
    latent = raw_sums[:, :L]
    mean_square = lax.optimization_barrier(jnp.mean(latent * latent, axis=1, keepdims=True))
    latent = latent * lax.rsqrt(mean_square + norm_eps) * gain[None, :]
    return jnp.concatenate([latent, rotate(raw_sums[:, L:], positions)], axis=1).astype(jnp.bfloat16)

def absorb(queries, up_weight):
    shaped = queries.reshape(queries.shape[0], H, QN + QR)
    absorbed = jnp.einsum('thn,hln->thl', shaped[:, :, :QN].astype(jnp.float32), up_weight[:, :, :QN].astype(jnp.float32)).astype(jnp.bfloat16)
    absorbed = lax.optimization_barrier(absorbed)
    return jnp.concatenate([absorbed, shaped[:, :, QN:]], axis=2)

def attend(full_query, keys, up_weight, block_kind):
    key_pos = jnp.arange(TOKENS, dtype=jnp.int32)
    score_scale = (QN + QR) ** (-0.5)
    keys_wide = keys.astype(jnp.float32)
    value_weight = up_weight[:, :, QN:].astype(jnp.float32)

    def one_block(block_index):
        queries_here = lax.dynamic_slice_in_dim(full_query, block_index * BLOCK, BLOCK, 0)
        kind_row = lax.dynamic_index_in_dim(block_kind, block_index, 0, keepdims=False)
        kind_keys = jnp.repeat(kind_row, BLOCK)
        query_pos = block_index * BLOCK + jnp.arange(BLOCK, dtype=jnp.int32)
        visible = (kind_keys[None, :] == 1) | (kind_keys[None, :] == 2) & (key_pos[None, :] <= query_pos[:, None])
        scores = jnp.einsum('thc,kc->htk', queries_here.astype(jnp.float32), keys_wide) * score_scale
        masked = jnp.where(visible[None], scores, -1e+30)
        row_max = lax.optimization_barrier(jnp.max(masked, axis=2, keepdims=True))
        exps = jnp.where(visible[None], jnp.exp(masked - row_max), 0.0)
        denominator = lax.optimization_barrier(jnp.sum(exps, axis=2))
        weights = lax.optimization_barrier(exps.astype(jnp.bfloat16))
        context = jnp.einsum('htk,kl->htl', weights.astype(jnp.float32), keys_wide[:, :L]) / denominator[:, :, None]
        context = lax.optimization_barrier(context.astype(jnp.bfloat16))
        mixed = jnp.einsum('htl,hlv->thv', context.astype(jnp.float32), value_weight).astype(jnp.bfloat16)
        return mixed.reshape(BLOCK, H * VD)
    blocks = lax.map(one_block, jnp.arange(NB, dtype=jnp.int32))
    return blocks.reshape(TOKENS, H * VD)

def score_copy(hidden, block_kind, queries, down_weight, gain, up_weight, positions):
    raw_sums = jnp.dot(hidden, down_weight, preferred_element_type=jnp.float32)
    keys = finish_keys(raw_sums, gain, positions)
    full_query = absorb(queries, up_weight)
    return attend(full_query, keys, up_weight, block_kind)

def reference(hidden, block_kind, policy_queries, policy_down, policy_gain, policy_up, frozen_queries, frozen_down, frozen_gain, frozen_up):
    positions = jnp.arange(TOKENS, dtype=jnp.int32).astype(jnp.float32)
    policy_out = score_copy(hidden, block_kind, policy_queries, policy_down, policy_gain, policy_up, positions)
    frozen_out = score_copy(hidden, block_kind, frozen_queries, frozen_down, frozen_gain, frozen_up, positions)
    return (policy_out, frozen_out)
```

```python
import functools

import jax
import jax.numpy as jnp
from jax import lax
from jax.experimental import pallas as pl
from jax.experimental.pallas import tpu as pltpu
from jax.sharding import Mesh, PartitionSpec as P

QN = 128
QR = 64
L = 512
VD = 128
BLOCK = 128
HEADS = 8
PIECE = 32
SLOTS = 32
TILE = 512
PER_TILE = TILE // PIECE
ROWS = 2 * BLOCK
MASKED = -3e38
START = -1e30
LOG2E = 1.4426950408889634
SCALE2 = (QN + QR) ** (-0.5) * LOG2E

norm_eps = 1e-06
rope_base = 10000.0

NAMES = ("z", "yl", "c", "yh", "x")
SIZES = (8, 2, 2, 2, 4)
CTX = ("z", "yl", "c")
FSDP = ("yh", "x")


def linear(z, yl, c, yh, x):
    return (((z * 2 + yl) * 2 + c) * 2 + yh) * 4 + x


def partners(move):
    pairs = []
    for z in range(8):
        for yl in range(2):
            for c in range(2):
                for yh in range(2):
                    for x in range(4):
                        z2, y2, x2, c2 = move(z, yh * 2 + yl, x, c)
                        pairs.append(
                            (linear(z, yl, c, yh, x), linear(z2, y2 % 2, c2, y2 // 2, x2))
                        )
    return pairs


SWAP_CORE = partners(lambda z, y, x, c: (z, y, x, 1 - c))
SWAP_YL = partners(lambda z, y, x, c: (z, y ^ 1, x, c))


def z_xor(k):
    return partners(lambda z, y, x, c: (z ^ k, y, x, c))


def first_axis(k):
    return partners(lambda z, y, x, c: (z, y ^ k, x, c) if c == 0 else (z, y, x ^ k, c))


def second_axis(k):
    return partners(lambda z, y, x, c: (z, y, x ^ k, c) if c == 0 else (z, y ^ k, x, c))


def send(value, pairs):
    return lax.ppermute(value, NAMES, pairs)


def rotate(values, positions):
    half_width = values.shape[1] // 2
    frequency = rope_base ** (-2.0 * jnp.arange(half_width, dtype=jnp.float32) / values.shape[1])
    angles = positions[:, None] * frequency[None, :]
    cosine = jnp.cos(angles)
    sine_term = jnp.sin(angles)
    first_half = values[:, :half_width]
    second_half = values[:, half_width:]
    return jnp.concatenate(
        [
            first_half * cosine - second_half * sine_term,
            second_half * cosine + first_half * sine_term,
        ],
        axis=1,
    )


def finish_keys(raw_sums, gain, positions):
    latent = raw_sums[:, :L]
    mean_square = jnp.mean(latent * latent, axis=1, keepdims=True)
    latent = latent * lax.rsqrt(mean_square + norm_eps) * gain[None, :]
    return jnp.concatenate([latent, rotate(raw_sums[:, L:], positions)], axis=1).astype(
        jnp.bfloat16
    )


def absorb_kernel(q_ref, up_ref, out_ref):
    for h in range(HEADS):
        left = h * (QN + QR)
        up = up_ref[:, h].reshape(L, QN + VD)
        absorbed = lax.dot_general(
            q_ref[:, left : left + QN],
            up[:, :QN],
            (((1,), (1,)), ((), ())),
            preferred_element_type=jnp.float32,
        )
        out_ref[h, :, :L] = absorbed.astype(jnp.bfloat16)
        out_ref[h, :, L:] = q_ref[:, left + QN : left + QN + QR]


def absorb(queries, up):
    return pl.pallas_call(
        absorb_kernel,
        out_shape=jax.ShapeDtypeStruct((HEADS, ROWS, L + QR), jnp.bfloat16),
        compiler_params=pltpu.CompilerParams(vmem_limit_bytes=48 * 2**20),
        cost_estimate=pl.CostEstimate(
            flops=2 * HEADS * ROWS * QN * L, bytes_accessed=6 * 2**20, transcendentals=0
        ),
        name="absorb",
    )(queries, up)


def attend_kernel(chunks, first, final, *refs):
    refs = list(refs)
    order_ref, tiles_ref, open_ref = refs[:3]
    cols_ref, rows_ref, q_ref = refs[3:6]
    key_refs = refs[6 : 6 + chunks]
    refs = refs[6 + chunks :]
    if not first:
        in_max, in_sum, in_acc = refs[:3]
        refs = refs[3:]
    if final:
        up_ref, out_ref = refs[:2]
        refs = refs[2:]
    else:
        out_max, out_sum, out_acc = refs[:3]
        refs = refs[3:]
    if final:
        out_max, out_sum, out_acc = refs[:3]
        refs = refs[3:]
    tile_ref, bias_ref = refs

    if first:
        out_max[...] = jnp.full_like(out_max, START)
        out_sum[...] = jnp.zeros_like(out_sum)
        out_acc[...] = jnp.zeros_like(out_acc)
    else:
        out_max[...] = in_max[...]
        out_sum[...] = in_sum[...]
        out_acc[...] = in_acc[...]

    def head_step(h, masked):
        scores = lax.dot_general(
            q_ref[h], tile_ref[...], (((1,), (1,)), ((), ())), preferred_element_type=jnp.float32
        )
        if masked:
            scores = scores + bias_ref[...]
        old = out_max[h]
        new = jnp.maximum(old, jnp.max(scores, axis=1, keepdims=True))
        exps = jnp.exp2((scores - new[:, :1]) * SCALE2)
        shrink = jnp.exp2((old - new) * SCALE2)
        out_max[h] = new
        out_sum[h] = out_sum[h] * shrink + jnp.sum(exps, axis=1, keepdims=True)
        mixed = jnp.dot(
            exps.astype(jnp.bfloat16), tile_ref[:, :L], preferred_element_type=jnp.float32
        )
        out_acc[h] = out_acc[h] * shrink[:, :1] + mixed

    for chunk in range(chunks):
        keys = key_refs[chunk]

        def one_tile(t, _, chunk=chunk, keys=keys):
            for s in range(PER_TILE):
                tile_ref[s * PIECE : (s + 1) * PIECE, :] = keys[order_ref[chunk, t * PER_TILE + s]]
            is_open = open_ref[chunk, t] == 1

            @pl.when(is_open)
            def _():
                def body(h, carry):
                    head_step(h, False)
                    return carry

                lax.fori_loop(0, HEADS, body, 0)

            @pl.when(jnp.logical_not(is_open))
            def _():
                cols = cols_ref[chunk, t]
                upper = lax.broadcasted_iota(jnp.int32, (ROWS, TILE), 0) < BLOCK
                kind = jnp.where(upper, cols[0:1, :], cols[1:2, :])
                seen = (kind == 1) | ((kind == 2) & (cols[2:3, :] <= rows_ref[:, :1]))
                bias_ref[...] = jnp.where(seen, 0.0, MASKED)

                def body(h, carry):
                    head_step(h, True)
                    return carry

                lax.fori_loop(0, HEADS, body, 0)

            return 0

        lax.fori_loop(0, tiles_ref[chunk], one_tile, 0)

    if final:
        for h in range(HEADS):
            context = (out_acc[h] / out_sum[h][:, :1]).astype(jnp.bfloat16)
            up = up_ref[:, h].reshape(L, QN + VD)
            out_ref[:, h * VD : (h + 1) * VD] = jnp.dot(
                context, up[:, QN:], preferred_element_type=jnp.float32
            ).astype(jnp.bfloat16)


def attend(plan, rows, query, keys, carry, up):
    order, tiles, is_open, cols = plan
    chunks = len(keys)
    first, final = carry is None, up is not None
    state = (
        jax.ShapeDtypeStruct((HEADS, ROWS, 128), jnp.float32),
        jax.ShapeDtypeStruct((HEADS, ROWS, 128), jnp.float32),
        jax.ShapeDtypeStruct((HEADS, ROWS, L), jnp.float32),
    )
    smem = pl.BlockSpec(memory_space=pltpu.SMEM)
    vmem = pl.BlockSpec(memory_space=pltpu.VMEM)
    operands = [order, tiles, is_open, cols, rows, query, *keys]
    specs = [smem] * 3 + [vmem] * (3 + chunks)
    if not first:
        operands += list(carry)
        specs += [vmem] * 3
    if final:
        operands.append(up)
        specs.append(vmem)
    scratch = [pltpu.VMEM((TILE, L + QR), jnp.bfloat16), pltpu.VMEM((ROWS, TILE), jnp.float32)]
    if final:
        out_shape = jax.ShapeDtypeStruct((ROWS, HEADS * VD), jnp.bfloat16)
        out_specs = vmem
        scratch = [pltpu.VMEM(s.shape, s.dtype) for s in state] + scratch
    else:
        out_shape = state
        out_specs = (vmem,) * 3
    return pl.pallas_call(
        functools.partial(attend_kernel, chunks, first, final),
        out_shape=out_shape,
        in_specs=specs,
        out_specs=out_specs,
        scratch_shapes=scratch,
        compiler_params=pltpu.CompilerParams(vmem_limit_bytes=56 * 2**20),
        cost_estimate=pl.CostEstimate(
            flops=chunks * 2 * HEADS * ROWS * 1024 * 1280,
            bytes_accessed=chunks * 2**20 + 8 * 2**20,
            transcendentals=chunks * HEADS * ROWS * 1024,
        ),
        name="attend",
    )(*operands)


def make_plan(kinds, core, z, y, x):
    rb = jnp.arange(4, dtype=jnp.int32)[:, None]
    slot = jnp.arange(SLOTS, dtype=jnp.int32)[None, :]
    ra, rz = slot // 8, slot % 8
    at_a = jnp.where(core == 0, y, x) ^ ra
    at_b = jnp.where(core == 0, x, y) ^ rb
    piece_y = jnp.where(core == 0, at_a + 0 * rb, at_b + 0 * ra)
    piece_x = jnp.where(core == 0, at_b + 0 * ra, at_a + 0 * rb)
    piece_z = z ^ rz
    block = piece_z * 4 + (piece_y % 2) * 2 + piece_y // 2
    block_ids = jnp.arange(32, dtype=jnp.int32)
    hit = (block[:, :, None] == block_ids).astype(jnp.int32)
    kind = jnp.sum(hit[None] * kinds[:, None, None, :], axis=3)
    start = block * BLOCK + piece_x * PIECE
    visible = (kind[0] > 0) | (kind[1] > 0)
    counts = jnp.sum(visible.astype(jnp.int32), axis=1)
    before = (slot[0][:, None] < slot[0][None, :]).astype(jnp.int32)
    rank = jnp.sum(visible.astype(jnp.int32)[:, :, None] * before[None], axis=1)
    place = (visible[:, None, :] & (rank[:, None, :] == slot[0][None, :, None])).astype(jnp.int32)
    order = jnp.sum(place * slot[0][None, None, :], axis=2)
    kind_at = jnp.sum(place[None] * kind[:, :, None, :], axis=3)
    start_at = jnp.sum(place * start[:, None, :], axis=2)
    tiles = (counts + PER_TILE - 1) // PER_TILE
    all_one = jnp.min(
        jnp.where(kind_at == 1, 1, 0).reshape(2, 4, SLOTS // PER_TILE, PER_TILE), axis=(0, 3)
    )
    offset = jnp.tile(jnp.arange(PIECE, dtype=jnp.int32), SLOTS)
    spread = jnp.stack(
        [
            jnp.repeat(kind_at[0], PIECE, axis=1),
            jnp.repeat(kind_at[1], PIECE, axis=1),
            jnp.repeat(start_at, PIECE, axis=1) + offset[None, :],
        ],
        axis=1,
    )
    spread = jnp.pad(spread, ((0, 0), (0, 5), (0, 0)))
    cols = spread.reshape(4, 8, SLOTS * PIECE // TILE, TILE).transpose(0, 2, 1, 3)
    return order, tiles, all_one, cols


def pick(plan, indices):
    return tuple(jnp.concatenate([part[i : i + 1] for i in indices], axis=0) for part in plan)


def shards(
    hidden,
    block_kind,
    policy_queries,
    policy_down,
    policy_gain,
    policy_up,
    frozen_queries,
    frozen_down,
    frozen_gain,
    frozen_up,
):
    core = lax.axis_index("c")
    z = lax.axis_index("z")
    yl = lax.axis_index("yl")
    yh = lax.axis_index("yh")
    x = lax.axis_index("x")
    y = yh * 2 + yl
    is_policy = core == 0

    def mine(policy, frozen):
        return jnp.where(is_policy, policy, frozen)

    def in_order(own, other):
        return jnp.where(is_policy, own, other), jnp.where(is_policy, other, own)

    other_hidden = send(hidden, SWAP_CORE)
    hidden_two = jnp.concatenate(in_order(hidden, other_hidden), axis=0)
    down = mine(policy_down, frozen_down)
    raw = jnp.dot(hidden_two, down, preferred_element_type=jnp.float32)
    parts = lax.all_to_all(raw.reshape(8, PIECE, L + QR), FSDP, 0, 0)
    raw_sum = jnp.sum(parts, axis=0)
    first_row = (z * 2 + yl) * ROWS + (yh * 4 + x) * PIECE
    positions = (first_row + jnp.arange(PIECE, dtype=jnp.int32)).astype(jnp.float32)
    own_keys = finish_keys(raw_sum, mine(policy_gain, frozen_gain), positions)

    own_up = mine(policy_up, frozen_up)
    other_up = send(mine(frozen_up, policy_up), SWAP_CORE)
    up_two = jnp.stack(in_order(own_up, other_up))
    far_up = send(up_two, SWAP_YL)
    low = jnp.where(yl == 0, up_two, far_up)
    high = jnp.where(yl == 0, far_up, up_two)
    up = lax.all_gather(jnp.concatenate([low, high], axis=0), "z", axis=0, tiled=True)

    own_queries = mine(policy_queries, frozen_queries)
    other_queries = send(mine(frozen_queries, policy_queries), SWAP_CORE)
    query = absorb(jnp.concatenate(in_order(own_queries, other_queries), axis=0), up)

    other_kind = send(block_kind, SWAP_CORE)
    plan = make_plan(jnp.concatenate(in_order(block_kind, other_kind), axis=0), core, z, y, x)
    rows = (z * 2 + yl) * ROWS + jnp.arange(ROWS, dtype=jnp.int32)
    rows = jnp.broadcast_to(rows[:, None], (ROWS, 128))

    held = own_keys[None]
    for step in (1, 2, 4):
        held = jnp.concatenate([held, send(held, z_xor(step))], axis=0)
    near1 = send(held, first_axis(1))
    near3 = send(held, first_axis(3))
    far_a = send(near3[:4], first_axis(1))
    far_b = send(near1[4:], first_axis(3))
    column = jnp.concatenate([held, near1, far_a, far_b, near3], axis=0)
    side1 = send(column, second_axis(1))
    side3 = send(column, second_axis(3))
    half = SLOTS // 2
    back_a = send(side3[:half], second_axis(1))
    back_b = send(side1[half:], second_axis(3))
    side2 = jnp.concatenate([back_a, back_b], axis=0)

    mixed = attend(plan, rows, query, [column, side1, side2, side3], None, up)

    upper, lower = mixed[:BLOCK], mixed[BLOCK:]
    kept = jnp.where(is_policy, upper, lower)
    got = send(jnp.where(is_policy, lower, upper), SWAP_CORE)
    return jnp.where(is_policy, kept, got), jnp.where(is_policy, got, kept)


def solution(mesh):
    fine = Mesh(mesh.devices.reshape(SIZES), NAMES)
    return jax.shard_map(
        shards,
        mesh=fine,
        in_specs=(
            P(CTX, FSDP),
            P(CTX, None),
            P(CTX, FSDP),
            P(FSDP, None),
            P(),
            P(FSDP, CTX, None),
            P(CTX, FSDP),
            P(FSDP, None),
            P(),
            P(FSDP, CTX, None),
        ),
        out_specs=(P(CTX, FSDP), P(CTX, FSDP)),
        check_vma=False,
    )
```

```python
import functools

import jax
import jax.numpy as jnp
from jax import lax
from jax.experimental import pallas as pl
from jax.experimental.pallas import tpu as pltpu
from jax.sharding import Mesh, PartitionSpec as P

QN = 128
QR = 64
L = 512
VD = 128
BLOCK = 128
HEADS = 8
PIECE = 32
SLOTS = 32
TILE = 512
PER_TILE = TILE // PIECE
GROUP = 2
TIED = 0
ROWS = 2 * BLOCK
MASKED = -3e38
START = -1e30
LOG2E = 1.4426950408889634
SCALE2 = (QN + QR) ** (-0.5) * LOG2E

norm_eps = 1e-06
rope_base = 10000.0

NAMES = ("z", "yl", "c", "yh", "x")
SIZES = (8, 2, 2, 2, 4)
CTX = ("z", "yl", "c")
FSDP = ("yh", "x")


def linear(z, yl, c, yh, x):
    return (((z * 2 + yl) * 2 + c) * 2 + yh) * 4 + x


def partners(move):
    pairs = []
    for z in range(8):
        for yl in range(2):
            for c in range(2):
                for yh in range(2):
                    for x in range(4):
                        z2, y2, x2, c2 = move(z, yh * 2 + yl, x, c)
                        pairs.append(
                            (linear(z, yl, c, yh, x), linear(z2, y2 % 2, c2, y2 // 2, x2))
                        )
    return pairs


SWAP_CORE = partners(lambda z, y, x, c: (z, y, x, 1 - c))
SWAP_YL = partners(lambda z, y, x, c: (z, y ^ 1, x, c))


def z_xor(k):
    return partners(lambda z, y, x, c: (z ^ k, y, x, c))


def z_ring(k):
    return partners(lambda z, y, x, c: ((z + k) % 8, y, x, c))


def first_axis(k):
    return partners(lambda z, y, x, c: (z, y ^ k, x, c) if c == 0 else (z, y, x ^ k, c))


def second_axis(k):
    return partners(lambda z, y, x, c: (z, y, x ^ k, c) if c == 0 else (z, y ^ k, x, c))


def send(value, pairs):
    return lax.ppermute(value, NAMES, pairs)


def rotate(values, positions):
    half_width = values.shape[1] // 2
    frequency = rope_base ** (-2.0 * jnp.arange(half_width, dtype=jnp.float32) / values.shape[1])
    angles = positions[:, None] * frequency[None, :]
    cosine = jnp.cos(angles)
    sine_term = jnp.sin(angles)
    first_half = values[:, :half_width]
    second_half = values[:, half_width:]
    return jnp.concatenate(
        [
            first_half * cosine - second_half * sine_term,
            second_half * cosine + first_half * sine_term,
        ],
        axis=1,
    )


def finish_keys(raw_sums, gain, positions):
    latent = raw_sums[:, :L]
    mean_square = jnp.mean(latent * latent, axis=1, keepdims=True)
    latent = latent * lax.rsqrt(mean_square + norm_eps) * gain[None, :]
    return jnp.concatenate([latent, rotate(raw_sums[:, L:], positions)], axis=1).astype(
        jnp.bfloat16
    )


SMEM = pl.BlockSpec(memory_space=pltpu.SMEM)
VMEM = pl.BlockSpec(memory_space=pltpu.VMEM)


def small_params():
    return pltpu.CompilerParams(vmem_limit_bytes=20 * 2**20)


def small_cost(flops, size):
    return pl.CostEstimate(flops=flops, bytes_accessed=size, transcendentals=0)


def join_kernel(sizes, *refs):
    out, top = refs[-1], 0
    for ref, size in zip(refs, sizes):
        out[top : top + size] = ref[...]
        top += size


def join(*arrays):
    sizes = [a.shape[0] for a in arrays]
    shape = (sum(sizes), *arrays[0].shape[1:])
    return pl.pallas_call(
        functools.partial(join_kernel, sizes),
        out_shape=jax.ShapeDtypeStruct(shape, arrays[0].dtype),
        in_specs=[VMEM] * len(arrays),
        out_specs=VMEM,
        compiler_params=small_params(),
        cost_estimate=small_cost(0, 2**20),
        name="join",
    )(*arrays)


def down_kernel(core_ref, own_ref, other_ref, policy_ref, frozen_ref, out_ref):
    core = core_ref[0]

    def both(weight_ref):
        weight = weight_ref[...]
        for ref, place in ((own_ref, core), (other_ref, 1 - core)):
            raw = lax.dot_general(
                ref[...], weight, (((1,), (1,)), ((), ())), preferred_element_type=jnp.float32
            )
            out_ref[pl.ds(place * 4, 4)] = raw.reshape(4, PIECE, L + QR)

    @pl.when(core == 0)
    def _():
        both(policy_ref)

    @pl.when(core == 1)
    def _():
        both(frozen_ref)


def project_down(core, own, other, policy, frozen):
    return pl.pallas_call(
        down_kernel,
        out_shape=jax.ShapeDtypeStruct((8, PIECE, L + QR), jnp.float32),
        in_specs=[SMEM] + [VMEM] * 4,
        out_specs=VMEM,
        compiler_params=small_params(),
        cost_estimate=small_cost(2 * ROWS * 896 * 576, 3 * 2**20),
        name="project_down",
    )(core[None], own, other, policy, frozen)


def absorb_kernel(place_ref, policy_ref, frozen_ref, other_ref, *refs):
    shard_refs, (out_ref, value_ref, up_ref, own_ref) = refs[:8], refs[8:]
    core, z, yl = place_ref[0], place_ref[1], place_ref[2]
    own_ref[...] = jnp.where(core == 0, policy_ref[...], frozen_ref[...])
    for shift in range(8):
        top = lax.rem(z + shift, 8) * (L // 8)
        for part in range(4):
            from_yl = lax.rem(yl + part // 2, 2)
            from_core = lax.rem(core + part % 2, 2)
            start = top + (from_yl * 2 + from_core) * 16
            place = pl.ds(pl.multiple_of(start, 16), 16)
            for h in range(HEADS):
                up_ref[h, place, :] = shard_refs[shift][part, h]
    for h in range(HEADS):
        left = h * (QN + QR)
        for ref, half in ((own_ref, core), (other_ref, 1 - core)):
            here = pl.ds(pl.multiple_of(h * ROWS + half * BLOCK, BLOCK), BLOCK)
            absorbed = lax.dot_general(
                ref[:, left : left + QN],
                up_ref[h, :, :QN],
                (((1,), (1,)), ((), ())),
                preferred_element_type=jnp.float32,
            )
            out_ref[here, :L] = absorbed.astype(jnp.bfloat16)
            out_ref[here, L:] = ref[:, left + QN : left + QN + QR]
        value_ref[h] = up_ref[h, :, QN:]


def absorb(place, policy, frozen, other, shards_by_shift):
    return pl.pallas_call(
        absorb_kernel,
        out_shape=(
            jax.ShapeDtypeStruct((HEADS * ROWS, L + QR), jnp.bfloat16),
            jax.ShapeDtypeStruct((HEADS, L, VD), jnp.bfloat16),
        ),
        in_specs=[SMEM] + [VMEM] * 11,
        out_specs=(VMEM, VMEM),
        scratch_shapes=[
            pltpu.VMEM((HEADS, L, QN + VD), jnp.bfloat16),
            pltpu.VMEM((BLOCK, HEADS * (QN + QR)), jnp.bfloat16),
        ],
        compiler_params=small_params(),
        cost_estimate=small_cost(2 * HEADS * ROWS * QN * L, 9 * 2**20),
        name="absorb",
    )(place, policy, frozen, other, *shards_by_shift)


CALLS = ((0,), (1, 3), (2,))
ORDER, KIND_0, KIND_1, BEGIN, COUNTS = range(5)


def plan_kernel(place_ref, own_ref, other_ref, out_ref, part_ref):
    core, z, yl, first, second = (place_ref[i] for i in range(5))
    left = 0
    for call, offsets in enumerate(CALLS):
        opens, partly = 0, left
        for index, rb in enumerate(offsets):

            def one_slot(inside, carry, call=call, index=index, rb=rb):
                opens, partly = carry
                rz = lax.rem(inside, 8)
                at_a, at_b = first ^ lax.div(inside, 8), second ^ rb
                piece_y = jnp.where(core == 0, at_a, at_b)
                piece_x = jnp.where(core == 0, at_b, at_a)
                piece_z = lax.rem(z + (rz & 6), 8) ^ (rz & 1)
                block = piece_z * 4 + (piece_y & 1) * 2 + (piece_y >> 1)
                own, other = own_ref[0, block], other_ref[0, block]
                kind_0 = jnp.where(core == 0, own, other)
                kind_1 = jnp.where(core == 0, other, own)
                begin = block * BLOCK + piece_x * PIECE
                is_open = (kind_0 == 1) & (kind_1 == 1)
                is_partly = ((kind_0 > 0) | (kind_1 > 0)) & jnp.logical_not(is_open)
                row = (index * SLOTS + inside, kind_0, kind_1, begin)

                @pl.when(is_open)
                def _():
                    for i, value in enumerate(row):
                        out_ref[call, i, opens] = value

                @pl.when(is_partly)
                def _():
                    for i, value in enumerate(row):
                        part_ref[i, partly] = value

                return opens + is_open.astype(jnp.int32), partly + is_partly.astype(jnp.int32)

            opens, partly = lax.fori_loop(0, SLOTS, one_slot, (opens, partly))

        def append(i, carry, call=call, opens=opens):
            for j in range(4):
                out_ref[call, j, opens + i] = part_ref[j, i]
            return carry

        lax.fori_loop(0, partly, append, 0)
        used = opens + partly
        if call < len(CALLS) - 1:
            tiles = lax.div(used, PER_TILE)
            left = used - tiles * PER_TILE

            def leave(i, carry, call=call, tiles=tiles):
                part_ref[0, i] = len(CALLS[call + 1]) * SLOTS + i
                for j in range(1, 4):
                    part_ref[j, i] = out_ref[call, j, tiles * PER_TILE + i]
                return carry

            lax.fori_loop(0, left, leave, 0)
        else:
            tiles = lax.div(used + (PER_TILE - 1), PER_TILE)

            def fill(i, carry, call=call):
                for j in range(4):
                    out_ref[call, j, i] = 0
                return carry

            lax.fori_loop(used, tiles * PER_TILE, fill, 0)
        out_ref[call, COUNTS, 0] = tiles
        out_ref[call, COUNTS, 1] = opens
        out_ref[call, COUNTS, 2] = used


def make_plan(place, own_kind, other_kind):
    return pl.pallas_call(
        plan_kernel,
        out_shape=jax.ShapeDtypeStruct((len(CALLS), 5, 128), jnp.int32),
        in_specs=[SMEM] * 3,
        out_specs=SMEM,
        scratch_shapes=[pltpu.SMEM((4, 128), jnp.int32)],
        compiler_params=small_params(),
        cost_estimate=small_cost(0, 4096),
        name="plan",
    )(place, own_kind, other_kind)


def attend_kernel(call, chunks, first, final, *refs):
    refs = list(refs)
    plan_ref, place_ref, q_ref, q_next_ref = refs[:4]
    key_refs = refs[4 : 4 + chunks]
    refs = refs[4 + chunks :]
    if not first:
        in_stat, in_acc = refs[:2]
        refs = refs[2:]
    if final:
        value_ref, keep_ref, send_ref, acc = refs[:4]
        refs = refs[4:]
    else:
        left_ref, out_stat, acc = refs[:3]
        refs = refs[3:]
    top, total, tile_ref, bias_ref, score_ref = refs
    step = pl.program_id(0)
    core, row_base = place_ref[0], (place_ref[1] * 2 + place_ref[2]) * ROWS
    tiles, opens = plan_ref[call, COUNTS, 0], plan_ref[call, COUNTS, 1]
    half = SLOTS // 2

    def has_unseen(t):
        return (t + 1) * PER_TILE > opens

    def score(query, t):
        keys = tile_ref[pl.ds(pl.multiple_of(t * TILE, TILE), TILE), :]
        return lax.dot_general(
            query, keys, (((1,), (1,)), ((), ())), preferred_element_type=jnp.float32
        )

    def piece_at(index):
        slot = plan_ref[call, ORDER, index]
        inside = lax.rem(slot, half)
        piece = key_refs[0][inside]
        for i in range(1, chunks):
            piece = jnp.where(slot >= i * half, key_refs[i][inside], piece)
        return piece

    if not final:

        @pl.when(step == 0)
        def _():
            def leave(index, carry):
                left_ref[index - tiles * PER_TILE] = piece_at(index)
                return carry

            lax.fori_loop(tiles * PER_TILE, plan_ref[call, COUNTS, 2], leave, 0)

    @pl.when(step == 0)
    def _():
        def gather(t, carry):
            for s in range(PER_TILE):
                place = pl.ds(pl.multiple_of(t * TILE + s * PIECE, PIECE), PIECE)
                tile_ref[place, :] = piece_at(t * PER_TILE + s)

            @pl.when(has_unseen(t))
            def _():
                lane = lax.broadcasted_iota(jnp.int32, (1, TILE), 1)
                kind_0 = jnp.zeros_like(lane)
                kind_1, begin = kind_0, kind_0
                for s in range(PER_TILE):
                    at = t * PER_TILE + s
                    here = lane // PIECE == s
                    kind_0 = jnp.where(here, plan_ref[call, KIND_0, at], kind_0)
                    kind_1 = jnp.where(here, plan_ref[call, KIND_1, at], kind_1)
                    begin = jnp.where(here, plan_ref[call, BEGIN, at], begin)
                key_row = begin + lane % PIECE
                row = lax.broadcasted_iota(jnp.int32, (ROWS, TILE), 0)
                kind = jnp.where(row < BLOCK, kind_0, kind_1)
                seen = (kind == 1) | ((kind == 2) & (key_row <= row + row_base))
                bias_ref[t] = jnp.where(seen, 0.0, MASKED)

            return carry

        lax.fori_loop(0, tiles, gather, 0)

        @pl.when(tiles > 0)
        def _():
            score_ref[0] = score(q_ref[...], 0)

    if first:
        top[...] = jnp.full_like(top, START)
        total[...] = jnp.zeros_like(total)
        acc[...] = jnp.zeros_like(acc)
    else:
        top[...] = jnp.broadcast_to(in_stat[:, :1], top.shape)
        total[...] = jnp.broadcast_to(in_stat[:, 64:65], total.shape)
        acc[...] = in_acc[...]

    begun = step * tiles

    def one_tile(t, carry):
        now = lax.rem(begun + t, 2)

        @pl.when(has_unseen(t))
        def _():
            for g in range(GROUP):
                here = slice(g * ROWS, (g + 1) * ROWS)
                score_ref[now, here, :] = score_ref[now, here, :] + bias_ref[t]

        scores = score_ref[now]
        last = t + 1 == tiles
        query = jnp.where(last, q_next_ref[...], q_ref[...])
        coming = score(query, jnp.where(last, 0, t + 1))
        old = top[...]
        new = jnp.maximum(old, jnp.max(scores, axis=1, keepdims=True))
        exps = jnp.exp2((scores - new[:, :1]) * SCALE2)
        shrink = jnp.exp2((old - new) * SCALE2)
        top[...] = new
        total[...] = total[...] * shrink + jnp.sum(exps, axis=1, keepdims=True)
        values = tile_ref[pl.ds(pl.multiple_of(t * TILE, TILE), TILE), :L]
        mixed = jnp.dot(exps.astype(jnp.bfloat16), values, preferred_element_type=jnp.float32)
        acc[...] = acc[...] * shrink[:, :1] + mixed
        score_ref[1 - now] = coming
        return carry

    lax.fori_loop(0, tiles, one_tile, 0)

    if final:
        for g in range(GROUP):
            for place, out in ((core, keep_ref), (1 - core, send_ref)):
                here = pl.ds(pl.multiple_of(g * ROWS + place * BLOCK, BLOCK), BLOCK)
                context = (acc[here, :] * (1.0 / total[here, :1])).astype(jnp.bfloat16)
                out[:, g * VD : (g + 1) * VD] = jnp.dot(
                    context, value_ref[g], preferred_element_type=jnp.float32
                ).astype(jnp.bfloat16)
    else:
        lane = lax.broadcasted_iota(jnp.int32, top.shape, 1)
        out_stat[...] = jnp.where(lane < 64, top[...], total[...])


def attend(call, plan, place, query, keys, carry, value):
    chunks = len(keys)
    first, final = carry is None, value is not None
    most = (chunks * SLOTS // 2 + PER_TILE - 1) // PER_TILE
    steps = HEADS // GROUP
    height = GROUP * ROWS
    def whole(array):
        return pl.BlockSpec(array.shape, lambda i: (0,) * len(array.shape))

    def by_step(width):
        return pl.BlockSpec((height, width), lambda i: (i, 0))

    q_next = pl.BlockSpec((height, L + QR), lambda i: (jnp.minimum(i + 1, steps - 1), 0))
    operands = [plan, place, query, query, *keys]
    specs = [SMEM] * 2 + [by_step(L + QR), q_next] + [whole(k) for k in keys]
    if not first:
        operands += list(carry)
        specs += [by_step(128), by_step(L)]
    scratch = [
        pltpu.VMEM((height, 128), jnp.float32),
        pltpu.VMEM((height, 128), jnp.float32),
        pltpu.VMEM((most * TILE, L + QR), jnp.bfloat16),
        pltpu.VMEM((most, ROWS, TILE), jnp.float32),
        pltpu.VMEM((2, height, TILE), jnp.float32),
    ]
    if final:
        operands.append(value)
        specs.append(pl.BlockSpec((GROUP, L, VD), lambda i: (i, 0, 0)))
        one = jax.ShapeDtypeStruct((BLOCK, HEADS * VD), jnp.bfloat16)
        out_shape = (one, one)
        out_specs = (pl.BlockSpec((BLOCK, GROUP * VD), lambda i: (0, i)),) * 2
        scratch = [pltpu.VMEM((height, L), jnp.float32)] + scratch
    else:
        left = jax.ShapeDtypeStruct((PER_TILE, PIECE, L + QR), jnp.bfloat16)
        out_shape = (
            left,
            jax.ShapeDtypeStruct((HEADS * ROWS, 128), jnp.float32),
            jax.ShapeDtypeStruct((HEADS * ROWS, L), jnp.float32),
        )
        out_specs = (whole(left), by_step(128), by_step(L))
    return pl.pallas_call(
        functools.partial(attend_kernel, call, chunks, first, final),
        grid=(steps,),
        out_shape=out_shape,
        in_specs=specs,
        out_specs=out_specs,
        scratch_shapes=scratch,
        compiler_params=pltpu.CompilerParams(vmem_limit_bytes=28 * 2**20),
        cost_estimate=pl.CostEstimate(
            flops=chunks * HEADS * ROWS * 1024 * 1280,
            bytes_accessed=chunks * 2**20 + 8 * 2**20,
            transcendentals=chunks * HEADS * ROWS * 512,
        ),
        name="attend",
    )(*operands)


def shards(
    hidden,
    block_kind,
    policy_queries,
    policy_down,
    policy_gain,
    policy_up,
    frozen_queries,
    frozen_down,
    frozen_gain,
    frozen_up,
):
    core = lax.axis_index("c")
    z = lax.axis_index("z")
    yl = lax.axis_index("yl")
    yh = lax.axis_index("yh")
    x = lax.axis_index("x")
    y = yh * 2 + yl
    is_policy = core == 0

    def mine(policy, frozen):
        return jnp.where(is_policy, policy, frozen)

    first_place, second_place = mine(y, x), mine(x, y)
    place = jnp.stack([core, z, yl, first_place, second_place])

    other_hidden = send(hidden, SWAP_CORE)
    own_up = mine(policy_up, frozen_up)
    other_up = send(mine(frozen_up, policy_up), SWAP_CORE)
    other_kind = send(block_kind, SWAP_CORE)
    raw = project_down(core, hidden, other_hidden, policy_down.T, frozen_down.T)
    raw, policy_queries, frozen_queries, other_kind, other_up = lax.optimization_barrier(
        (raw, policy_queries, frozen_queries, other_kind, other_up)
    )
    parts = lax.all_to_all(raw, FSDP, 0, 0)

    plan = make_plan(place, block_kind, other_kind)

    up_two = jnp.stack([own_up, other_up])
    up_here = jnp.concatenate([up_two, send(up_two, SWAP_YL)], axis=0)
    below, above = [up_here], [up_here]
    for step in range(3):
        below.append(send(below[-1], z_ring(1)))
        above.append(send(above[-1], z_ring(-1)))
        if step == TIED:
            parts, plan, below[-1], above[-1] = lax.optimization_barrier(
                (parts, plan, below[-1], above[-1])
            )
    opposite = send(below[3], z_ring(1))
    by_shift = [up_here, above[1], above[2], above[3], opposite, below[3], below[2], below[1]]

    raw_sum = jnp.sum(parts, axis=0)
    first_row = (z * 2 + yl) * ROWS + (yh * 4 + x) * PIECE
    positions = (first_row + jnp.arange(PIECE, dtype=jnp.int32)).astype(jnp.float32)
    own_keys = finish_keys(raw_sum, mine(policy_gain, frozen_gain), positions)

    other_queries = send(mine(frozen_queries, policy_queries), SWAP_CORE)
    query, value = absorb(place, policy_queries, frozen_queries, other_queries, by_shift)

    pair = jnp.stack([own_keys, send(own_keys, z_xor(1))])
    pair_below, pair_above = send(pair, z_ring(2)), send(pair, z_ring(-2))
    pair_far = send(pair_below, z_ring(2))
    held = join(pair, pair_above, pair_far, pair_below)
    near1 = send(held, first_axis(1))
    near3 = send(held, first_axis(3))
    far = send(near3, first_axis(1))
    low = join(held, near1)
    side3_low = send(low, second_axis(3))
    side1_low = send(low, second_axis(1))
    far, query, value = lax.optimization_barrier((far, query, value))
    high = join(far, near3)
    side1_high = send(high, second_axis(1))
    side3_high = send(high, second_axis(3))
    left, *carry = attend(0, plan, place, query, [low, high], None, None)
    side2_low = send(side3_low, second_axis(1))
    side2_high = send(side1_high, second_axis(3))
    sides = [side1_low, side1_high, side3_low, side3_high]
    left, *carry = attend(1, plan, place, query, [*sides, left], carry, None)
    kept, sent = attend(2, plan, place, query, [side2_low, side2_high, left], carry, value)

    got = send(sent, SWAP_CORE)
    return jnp.where(is_policy, kept, got), jnp.where(is_policy, got, kept)


def solution(mesh):
    fine = Mesh(mesh.devices.reshape(SIZES), NAMES)
    return jax.shard_map(
        shards,
        mesh=fine,
        in_specs=(
            P(CTX, FSDP),
            P(CTX, None),
            P(CTX, FSDP),
            P(FSDP, None),
            P(),
            P(FSDP, CTX, None),
            P(CTX, FSDP),
            P(FSDP, None),
            P(),
            P(FSDP, CTX, None),
        ),
        out_specs=(P(CTX, FSDP), P(CTX, FSDP)),
        check_vma=False,
    )
```

```python
import functools

import jax
import jax.numpy as jnp
from jax import lax
from jax.experimental import pallas as pl
from jax.experimental.pallas import tpu as pltpu
from jax.sharding import Mesh, PartitionSpec as P

QN = 128
QR = 64
L = 512
VD = 128
BLOCK = 128
HEADS = 8
PIECE = 32
SLOTS = 32
TILE = 512
PER_TILE = TILE // PIECE
GROUP = 2
TIED = 0
ROWS = 2 * BLOCK
MASKED = -3e38
START = -1e30
LOG2E = 1.4426950408889634
SCALE2 = (QN + QR) ** (-0.5) * LOG2E

norm_eps = 1e-06
rope_base = 10000.0

NAMES = ("z", "yl", "c", "yh", "x")
SIZES = (8, 2, 2, 2, 4)
CTX = ("z", "yl", "c")
FSDP = ("yh", "x")


def linear(z, yl, c, yh, x):
    return (((z * 2 + yl) * 2 + c) * 2 + yh) * 4 + x


def partners(move):
    pairs = []
    for z in range(8):
        for yl in range(2):
            for c in range(2):
                for yh in range(2):
                    for x in range(4):
                        z2, y2, x2, c2 = move(z, yh * 2 + yl, x, c)
                        pairs.append(
                            (linear(z, yl, c, yh, x), linear(z2, y2 % 2, c2, y2 // 2, x2))
                        )
    return pairs


SWAP_CORE = partners(lambda z, y, x, c: (z, y, x, 1 - c))
SWAP_YL = partners(lambda z, y, x, c: (z, y ^ 1, x, c))


def z_xor(k):
    return partners(lambda z, y, x, c: (z ^ k, y, x, c))


def z_ring(k):
    return partners(lambda z, y, x, c: ((z + k) % 8, y, x, c))


def first_axis(k):
    return partners(lambda z, y, x, c: (z, y ^ k, x, c) if c == 0 else (z, y, x ^ k, c))


def second_axis(k):
    return partners(lambda z, y, x, c: (z, y, x ^ k, c) if c == 0 else (z, y ^ k, x, c))


def send(value, pairs):
    return lax.ppermute(value, NAMES, pairs)


def rotate(values, positions):
    half_width = values.shape[1] // 2
    frequency = rope_base ** (-2.0 * jnp.arange(half_width, dtype=jnp.float32) / values.shape[1])
    angles = positions[:, None] * frequency[None, :]
    cosine = jnp.cos(angles)
    sine_term = jnp.sin(angles)
    first_half = values[:, :half_width]
    second_half = values[:, half_width:]
    return jnp.concatenate(
        [
            first_half * cosine - second_half * sine_term,
            second_half * cosine + first_half * sine_term,
        ],
        axis=1,
    )


def finish_keys(raw_sums, gain, positions):
    latent = raw_sums[:, :L]
    mean_square = jnp.mean(latent * latent, axis=1, keepdims=True)
    latent = latent * lax.rsqrt(mean_square + norm_eps) * gain[None, :]
    return jnp.concatenate([latent, rotate(raw_sums[:, L:], positions)], axis=1).astype(
        jnp.bfloat16
    )


SMEM = pl.BlockSpec(memory_space=pltpu.SMEM)
VMEM = pl.BlockSpec(memory_space=pltpu.VMEM)


def small_params():
    return pltpu.CompilerParams(vmem_limit_bytes=20 * 2**20)


def small_cost(flops, size):
    return pl.CostEstimate(flops=flops, bytes_accessed=size, transcendentals=0)


def join_kernel(sizes, *refs):
    out, top = refs[-1], 0
    for ref, size in zip(refs, sizes):
        out[top : top + size] = ref[...]
        top += size


def join(*arrays):
    sizes = [a.shape[0] for a in arrays]
    shape = (sum(sizes), *arrays[0].shape[1:])
    return pl.pallas_call(
        functools.partial(join_kernel, sizes),
        out_shape=jax.ShapeDtypeStruct(shape, arrays[0].dtype),
        in_specs=[VMEM] * len(arrays),
        out_specs=VMEM,
        compiler_params=small_params(),
        cost_estimate=small_cost(0, 2**20),
        name="join",
    )(*arrays)


def down_kernel(core_ref, own_ref, other_ref, policy_ref, frozen_ref, out_ref):
    core = core_ref[0]

    def both(weight_ref):
        weight = weight_ref[...]
        for ref, place in ((own_ref, core), (other_ref, 1 - core)):
            raw = lax.dot_general(
                ref[...], weight, (((1,), (1,)), ((), ())), preferred_element_type=jnp.float32
            )
            out_ref[pl.ds(place * 4, 4)] = raw.reshape(4, PIECE, L + QR)

    @pl.when(core == 0)
    def _():
        both(policy_ref)

    @pl.when(core == 1)
    def _():
        both(frozen_ref)


def project_down(core, own, other, policy, frozen):
    return pl.pallas_call(
        down_kernel,
        out_shape=jax.ShapeDtypeStruct((8, PIECE, L + QR), jnp.float32),
        in_specs=[SMEM] + [VMEM] * 4,
        out_specs=VMEM,
        compiler_params=small_params(),
        cost_estimate=small_cost(2 * ROWS * 896 * 576, 3 * 2**20),
        name="project_down",
    )(core[None], own, other, policy, frozen)


def absorb_kernel(place_ref, policy_ref, frozen_ref, other_ref, *refs):
    shard_refs, (out_ref, value_ref, up_ref, own_ref) = refs[:8], refs[8:]
    core, z, yl = place_ref[0], place_ref[1], place_ref[2]
    own_ref[...] = jnp.where(core == 0, policy_ref[...], frozen_ref[...])
    for shift in range(8):
        top = lax.rem(z + shift, 8) * (L // 8)
        for part in range(4):
            from_yl = lax.rem(yl + part // 2, 2)
            from_core = lax.rem(core + part % 2, 2)
            start = top + (from_yl * 2 + from_core) * 16
            place = pl.ds(pl.multiple_of(start, 16), 16)
            for h in range(HEADS):
                up_ref[h, place, :] = shard_refs[shift][part, h]
    for h in range(HEADS):
        left = h * (QN + QR)
        for ref, half in ((own_ref, core), (other_ref, 1 - core)):
            here = pl.ds(pl.multiple_of(h * ROWS + half * BLOCK, BLOCK), BLOCK)
            absorbed = lax.dot_general(
                ref[:, left : left + QN],
                up_ref[h, :, :QN],
                (((1,), (1,)), ((), ())),
                preferred_element_type=jnp.float32,
            )
            out_ref[here, :L] = absorbed.astype(jnp.bfloat16)
            out_ref[here, L:] = ref[:, left + QN : left + QN + QR]
        value_ref[h] = up_ref[h, :, QN:]


def absorb(place, policy, frozen, other, shards_by_shift):
    return pl.pallas_call(
        absorb_kernel,
        out_shape=(
            jax.ShapeDtypeStruct((HEADS * ROWS, L + QR), jnp.bfloat16),
            jax.ShapeDtypeStruct((HEADS, L, VD), jnp.bfloat16),
        ),
        in_specs=[SMEM] + [VMEM] * 11,
        out_specs=(VMEM, VMEM),
        scratch_shapes=[
            pltpu.VMEM((HEADS, L, QN + VD), jnp.bfloat16),
            pltpu.VMEM((BLOCK, HEADS * (QN + QR)), jnp.bfloat16),
        ],
        compiler_params=small_params(),
        cost_estimate=small_cost(2 * HEADS * ROWS * QN * L, 9 * 2**20),
        name="absorb",
    )(place, policy, frozen, other, *shards_by_shift)


CALLS = ((0,), (1, 3), (2,))
TILES, OPENS, USED = 124, 125, 126


def pack(slot, kind_0, kind_1, begin):
    return slot | (kind_0 << 8) | (kind_1 << 10) | (begin << 12)


def plan_kernel(place_ref, own_ref, other_ref, out_ref, part_ref, kind_ref):
    core, z, yl, first, second = (place_ref[i] for i in range(5))
    is_first = core == 0

    def one_block(block, carry):
        own, other = own_ref[0, block], other_ref[0, block]
        kind_0, kind_1 = jnp.where(is_first, own, other), jnp.where(is_first, other, own)
        kind_ref[block] = pack(0, kind_0, kind_1, block * BLOCK)
        return carry

    lax.fori_loop(0, 32, one_block, 0)
    both_open = pack(0, 1, 1, 0)
    any_kind = pack(0, 3, 3, 0)
    counts = []
    for call, offsets in enumerate(CALLS):
        opens, partly = 0, 0
        for index, rb in enumerate(offsets):
            at_b = second ^ rb
            for ra in range(4):
                at_a = first ^ ra
                piece_y = jnp.where(is_first, at_a, at_b)
                piece_x = jnp.where(is_first, at_b, at_a)
                shift = (piece_y & 1) * 2 + (piece_y >> 1)
                extra = pack(index * SLOTS + ra * 8, 0, 0, piece_x * PIECE)
                for rz in range(8):
                    piece_z = lax.rem(z + (rz & 6), 8) ^ (rz & 1)
                    item = kind_ref[piece_z * 4 + shift] + (extra + rz)
                    kinds = item & any_kind
                    is_open = kinds == both_open
                    out_ref[call, opens] = item
                    part_ref[call, partly] = item
                    opens = opens + is_open.astype(jnp.int32)
                    partly = partly + (jnp.logical_not(is_open) & (kinds != 0)).astype(jnp.int32)
        counts.append((opens, partly))

    moved = 0
    for call, (opens, partly) in enumerate(counts):

        def append(i, carry, call=call, opens=opens):
            out_ref[call, opens + i] = part_ref[call, i]
            return carry

        lax.fori_loop(0, partly, append, 0)
        used = opens + partly
        if call:

            def take(i, carry, call=call, used=used, start=start):
                item = out_ref[call - 1, start + i]
                slot = len(CALLS[call]) * SLOTS + i
                out_ref[call, used + i] = (item & ~255) | slot
                return carry

            lax.fori_loop(0, moved, take, 0)
            used = used + moved
        tiles = lax.div(used + (PER_TILE - 1), PER_TILE)
        if call < len(CALLS) - 1:
            spare = lax.rem(used, PER_TILE)
            coming = counts[call + 1][0] + counts[call + 1][1]
            room = lax.rem(PER_TILE - lax.rem(coming, PER_TILE), PER_TILE)
            moved = jnp.where(spare <= room, spare, 0)
            out_ref[call, USED] = used
            used = used - moved
            tiles = lax.div(used + (PER_TILE - 1), PER_TILE)
            start = used

        def fill(i, carry, call=call):
            out_ref[call, i] = 0
            return carry

        if call < len(CALLS) - 1:
            lax.fori_loop(jnp.where(moved > 0, tiles * PER_TILE, used), tiles * PER_TILE, fill, 0)
        else:
            lax.fori_loop(used, tiles * PER_TILE, fill, 0)
        out_ref[call, TILES] = tiles
        out_ref[call, OPENS] = opens


def make_plan(place, own_kind, other_kind):
    return pl.pallas_call(
        plan_kernel,
        out_shape=jax.ShapeDtypeStruct((len(CALLS), 128), jnp.int32),
        in_specs=[SMEM] * 3,
        out_specs=SMEM,
        scratch_shapes=[pltpu.SMEM((3, 128), jnp.int32), pltpu.SMEM((32,), jnp.int32)],
        compiler_params=small_params(),
        cost_estimate=small_cost(0, 4096),
        name="plan",
    )(place, own_kind, other_kind)


def attend_kernel(call, chunks, first, final, *refs):
    refs = list(refs)
    plan_ref, place_ref, q_ref, q_next_ref = refs[:4]
    key_refs = refs[4 : 4 + chunks]
    refs = refs[4 + chunks :]
    if not first:
        in_stat, in_acc = refs[:2]
        refs = refs[2:]
    if final:
        value_ref, keep_ref, send_ref, acc = refs[:4]
        refs = refs[4:]
    else:
        left_ref, out_stat, acc = refs[:3]
        refs = refs[3:]
    top, total, tile_ref, bias_ref, score_ref = refs
    step = pl.program_id(0)
    core, row_base = place_ref[0], (place_ref[1] * 2 + place_ref[2]) * ROWS
    tiles, opens = plan_ref[call, TILES], plan_ref[call, OPENS]
    half = SLOTS // 2

    def has_unseen(t):
        return (t + 1) * PER_TILE > opens

    def score(query, t):
        keys = tile_ref[pl.ds(pl.multiple_of(t * TILE, TILE), TILE), :]
        return lax.dot_general(
            query, keys, (((1,), (1,)), ((), ())), preferred_element_type=jnp.float32
        )

    def piece_at(index):
        slot = plan_ref[call, index] & 255
        inside = lax.rem(slot, half)
        piece = key_refs[0][inside]
        for i in range(1, chunks):
            piece = jnp.where(slot >= i * half, key_refs[i][inside], piece)
        return piece

    if not final:

        @pl.when(step == 0)
        def _():
            def leave(index, carry):
                left_ref[index - tiles * PER_TILE] = piece_at(index)
                return carry

            lax.fori_loop(tiles * PER_TILE, plan_ref[call, USED], leave, 0)

    @pl.when(step == 0)
    def _():
        def gather(t, carry):
            for s in range(PER_TILE):
                place = pl.ds(pl.multiple_of(t * TILE + s * PIECE, PIECE), PIECE)
                tile_ref[place, :] = piece_at(t * PER_TILE + s)

            @pl.when(has_unseen(t))
            def _():
                lane = lax.broadcasted_iota(jnp.int32, (1, TILE), 1)
                kind_0 = jnp.zeros_like(lane)
                kind_1, begin = kind_0, kind_0
                for s in range(PER_TILE):
                    item = plan_ref[call, t * PER_TILE + s]
                    here = lane // PIECE == s
                    kind_0 = jnp.where(here, (item >> 8) & 3, kind_0)
                    kind_1 = jnp.where(here, (item >> 10) & 3, kind_1)
                    begin = jnp.where(here, item >> 12, begin)
                key_row = begin + lane % PIECE
                row = lax.broadcasted_iota(jnp.int32, (ROWS, TILE), 0)
                kind = jnp.where(row < BLOCK, kind_0, kind_1)
                seen = (kind == 1) | ((kind == 2) & (key_row <= row + row_base))
                bias_ref[t] = jnp.where(seen, 0.0, MASKED)

            return carry

        lax.fori_loop(0, tiles, gather, 0)

        @pl.when(tiles > 0)
        def _():
            score_ref[0] = score(q_ref[...], 0)

    if first:
        top[...] = jnp.full_like(top, START)
        total[...] = jnp.zeros_like(total)
        acc[...] = jnp.zeros_like(acc)
    else:
        top[...] = jnp.broadcast_to(in_stat[:, :1], top.shape)
        total[...] = jnp.broadcast_to(in_stat[:, 64:65], total.shape)
        acc[...] = in_acc[...]

    begun = step * tiles

    def one_tile(t, carry):
        now = lax.rem(begun + t, 2)

        @pl.when(has_unseen(t))
        def _():
            for g in range(GROUP):
                here = slice(g * ROWS, (g + 1) * ROWS)
                score_ref[now, here, :] = score_ref[now, here, :] + bias_ref[t]

        scores = score_ref[now]
        last = t + 1 == tiles
        query = jnp.where(last, q_next_ref[...], q_ref[...])
        coming = score(query, jnp.where(last, 0, t + 1))
        old = top[...]
        new = jnp.maximum(old, jnp.max(scores, axis=1, keepdims=True))
        exps = jnp.exp2((scores - new[:, :1]) * SCALE2)
        shrink = jnp.exp2((old - new) * SCALE2)
        top[...] = new
        total[...] = total[...] * shrink + jnp.sum(exps, axis=1, keepdims=True)
        values = tile_ref[pl.ds(pl.multiple_of(t * TILE, TILE), TILE), :L]
        mixed = jnp.dot(exps.astype(jnp.bfloat16), values, preferred_element_type=jnp.float32)
        acc[...] = acc[...] * shrink[:, :1] + mixed
        score_ref[1 - now] = coming
        return carry

    lax.fori_loop(0, tiles, one_tile, 0)

    if final:
        context = (acc[...] * (1.0 / total[:, :1])).astype(jnp.bfloat16)
        for g in range(GROUP):
            mixed = jnp.dot(
                context[g * ROWS : (g + 1) * ROWS], value_ref[g], preferred_element_type=jnp.float32
            ).astype(jnp.bfloat16)
            left, right = mixed[:BLOCK], mixed[BLOCK:]
            columns = slice(g * VD, (g + 1) * VD)
            keep_ref[:, columns] = jnp.where(core == 0, left, right)
            send_ref[:, columns] = jnp.where(core == 0, right, left)
    else:
        lane = lax.broadcasted_iota(jnp.int32, top.shape, 1)
        out_stat[...] = jnp.where(lane < 64, top[...], total[...])


def attend(call, plan, place, query, keys, carry, value):
    chunks = len(keys)
    first, final = carry is None, value is not None
    most = (chunks * SLOTS // 2 + PER_TILE - 1) // PER_TILE
    steps = HEADS // GROUP
    height = GROUP * ROWS
    def whole(array):
        return pl.BlockSpec(array.shape, lambda i: (0,) * len(array.shape))

    def by_step(width):
        return pl.BlockSpec((height, width), lambda i: (i, 0))

    q_next = pl.BlockSpec((height, L + QR), lambda i: (jnp.minimum(i + 1, steps - 1), 0))
    operands = [plan, place, query, query, *keys]
    specs = [SMEM] * 2 + [by_step(L + QR), q_next] + [whole(k) for k in keys]
    if not first:
        operands += list(carry)
        specs += [by_step(128), by_step(L)]
    scratch = [
        pltpu.VMEM((height, 128), jnp.float32),
        pltpu.VMEM((height, 128), jnp.float32),
        pltpu.VMEM((most * TILE, L + QR), jnp.bfloat16),
        pltpu.VMEM((most, ROWS, TILE), jnp.float32),
        pltpu.VMEM((2, height, TILE), jnp.float32),
    ]
    if final:
        operands.append(value)
        specs.append(pl.BlockSpec((GROUP, L, VD), lambda i: (i, 0, 0)))
        one = jax.ShapeDtypeStruct((BLOCK, HEADS * VD), jnp.bfloat16)
        out_shape = (one, one)
        out_specs = (pl.BlockSpec((BLOCK, GROUP * VD), lambda i: (0, i)),) * 2
        scratch = [pltpu.VMEM((height, L), jnp.float32)] + scratch
    else:
        left = jax.ShapeDtypeStruct((PER_TILE, PIECE, L + QR), jnp.bfloat16)
        out_shape = (
            left,
            jax.ShapeDtypeStruct((HEADS * ROWS, 128), jnp.float32),
            jax.ShapeDtypeStruct((HEADS * ROWS, L), jnp.float32),
        )
        out_specs = (whole(left), by_step(128), by_step(L))
    return pl.pallas_call(
        functools.partial(attend_kernel, call, chunks, first, final),
        grid=(steps,),
        out_shape=out_shape,
        in_specs=specs,
        out_specs=out_specs,
        scratch_shapes=scratch,
        compiler_params=pltpu.CompilerParams(vmem_limit_bytes=28 * 2**20),
        cost_estimate=pl.CostEstimate(
            flops=chunks * HEADS * ROWS * 1024 * 1280,
            bytes_accessed=chunks * 2**20 + 8 * 2**20,
            transcendentals=chunks * HEADS * ROWS * 512,
        ),
        name="attend",
    )(*operands)


def shards(
    hidden,
    block_kind,
    policy_queries,
    policy_down,
    policy_gain,
    policy_up,
    frozen_queries,
    frozen_down,
    frozen_gain,
    frozen_up,
):
    core = lax.axis_index("c")
    z = lax.axis_index("z")
    yl = lax.axis_index("yl")
    yh = lax.axis_index("yh")
    x = lax.axis_index("x")
    y = yh * 2 + yl
    is_policy = core == 0

    def mine(policy, frozen):
        return jnp.where(is_policy, policy, frozen)

    first_place, second_place = mine(y, x), mine(x, y)
    place = jnp.stack([core, z, yl, first_place, second_place])

    other_hidden = send(hidden, SWAP_CORE)
    own_up = mine(policy_up, frozen_up)
    other_up = send(mine(frozen_up, policy_up), SWAP_CORE)
    other_kind = send(block_kind, SWAP_CORE)
    raw = project_down(core, hidden, other_hidden, policy_down.T, frozen_down.T)
    raw, policy_queries, frozen_queries, other_kind, other_up = lax.optimization_barrier(
        (raw, policy_queries, frozen_queries, other_kind, other_up)
    )
    parts = lax.all_to_all(raw, FSDP, 0, 0)

    plan = make_plan(place, block_kind, other_kind)

    up_two = jnp.stack([own_up, other_up])
    up_here = jnp.concatenate([up_two, send(up_two, SWAP_YL)], axis=0)
    below, above = [up_here], [up_here]
    below.append(send(up_here, z_ring(1)))
    above.append(send(up_here, z_ring(-1)))
    parts, plan, below[1], above[1] = lax.optimization_barrier((parts, plan, below[1], above[1]))

    raw_sum = jnp.sum(parts, axis=0)
    first_row = (z * 2 + yl) * ROWS + (yh * 4 + x) * PIECE
    positions = (first_row + jnp.arange(PIECE, dtype=jnp.int32)).astype(jnp.float32)
    own_keys = finish_keys(raw_sum, mine(policy_gain, frozen_gain), positions)

    pair = jnp.stack([own_keys, send(own_keys, z_xor(1))])
    pair, below[1], above[1] = lax.optimization_barrier((pair, below[1], above[1]))
    for step in (1, 2):
        below.append(send(below[step], z_ring(1)))
        above.append(send(above[step], z_ring(-1)))
    opposite = send(below[3], z_ring(1))
    by_shift = [up_here, above[1], above[2], above[3], opposite, below[3], below[2], below[1]]

    other_queries = send(mine(frozen_queries, policy_queries), SWAP_CORE)
    query, value = absorb(place, policy_queries, frozen_queries, other_queries, by_shift)

    pair_below, pair_above = send(pair, z_ring(2)), send(pair, z_ring(-2))
    pair_far = send(pair, z_ring(4))
    held = join(pair, pair_above, pair_far, pair_below)
    near1 = send(held, first_axis(1))
    near3 = send(held, first_axis(3))
    far = send(held, first_axis(2))
    low = join(held, near1)
    side3_low = send(low, second_axis(3))
    side1_low = send(low, second_axis(1))
    high = join(far, near3)
    side1_high = send(high, second_axis(1))
    side3_high = send(high, second_axis(3))
    left, *carry = attend(0, plan, place, query, [low, high], None, None)
    side2_low = send(side3_low, second_axis(1))
    side2_high = send(side1_high, second_axis(3))
    sides = [side1_low, side1_high, side3_low, side3_high]
    left, *carry = attend(1, plan, place, query, [*sides, left], carry, None)
    kept, sent = attend(2, plan, place, query, [side2_low, side2_high, left], carry, value)

    got = send(sent, SWAP_CORE)
    return jnp.where(is_policy, kept, got), jnp.where(is_policy, got, kept)


def solution(mesh):
    fine = Mesh(mesh.devices.reshape(SIZES), NAMES)
    return jax.shard_map(
        shards,
        mesh=fine,
        in_specs=(
            P(CTX, FSDP),
            P(CTX, None),
            P(CTX, FSDP),
            P(FSDP, None),
            P(),
            P(FSDP, CTX, None),
            P(CTX, FSDP),
            P(FSDP, None),
            P(),
            P(FSDP, CTX, None),
        ),
        out_specs=(P(CTX, FSDP), P(CTX, FSDP)),
        check_vma=False,
    )
```

```python
import functools

import jax
import jax.numpy as jnp
from jax import lax
from jax.experimental import pallas as pl
from jax.experimental.pallas import tpu as pltpu
from jax.sharding import Mesh, PartitionSpec as P

QN = 128
QR = 64
L = 512
VD = 128
BLOCK = 128
HEADS = 8
PIECE = 32
SLOTS = 32
TILE = 512
PER_TILE = TILE // PIECE
GROUP = 2
TIED = 0
ROWS = 2 * BLOCK
MASKED = -3e38
START = -1e30
LOG2E = 1.4426950408889634
SCALE2 = (QN + QR) ** (-0.5) * LOG2E

norm_eps = 1e-06
rope_base = 10000.0

NAMES = ("z", "yl", "c", "yh", "x")
SIZES = (8, 2, 2, 2, 4)
CTX = ("z", "yl", "c")
FSDP = ("yh", "x")


def linear(z, yl, c, yh, x):
    return (((z * 2 + yl) * 2 + c) * 2 + yh) * 4 + x


def partners(move):
    pairs = []
    for z in range(8):
        for yl in range(2):
            for c in range(2):
                for yh in range(2):
                    for x in range(4):
                        z2, y2, x2, c2 = move(z, yh * 2 + yl, x, c)
                        pairs.append(
                            (linear(z, yl, c, yh, x), linear(z2, y2 % 2, c2, y2 // 2, x2))
                        )
    return pairs


SWAP_CORE = partners(lambda z, y, x, c: (z, y, x, 1 - c))
SWAP_YL = partners(lambda z, y, x, c: (z, y ^ 1, x, c))


def z_xor(k):
    return partners(lambda z, y, x, c: (z ^ k, y, x, c))


def z_ring(k):
    return partners(lambda z, y, x, c: ((z + k) % 8, y, x, c))


def first_axis(k):
    return partners(lambda z, y, x, c: (z, y ^ k, x, c) if c == 0 else (z, y, x ^ k, c))


def second_axis(k):
    return partners(lambda z, y, x, c: (z, y, x ^ k, c) if c == 0 else (z, y ^ k, x, c))


def send(value, pairs):
    return lax.ppermute(value, NAMES, pairs)


def rotate(values, positions):
    half_width = values.shape[1] // 2
    frequency = rope_base ** (-2.0 * jnp.arange(half_width, dtype=jnp.float32) / values.shape[1])
    angles = positions[:, None] * frequency[None, :]
    cosine = jnp.cos(angles)
    sine_term = jnp.sin(angles)
    first_half = values[:, :half_width]
    second_half = values[:, half_width:]
    return jnp.concatenate(
        [
            first_half * cosine - second_half * sine_term,
            second_half * cosine + first_half * sine_term,
        ],
        axis=1,
    )


def finish_keys(raw_sums, gain, positions):
    latent = raw_sums[:, :L]
    mean_square = jnp.mean(latent * latent, axis=1, keepdims=True)
    latent = latent * lax.rsqrt(mean_square + norm_eps) * gain[None, :]
    return jnp.concatenate([latent, rotate(raw_sums[:, L:], positions)], axis=1).astype(
        jnp.bfloat16
    )


SMEM = pl.BlockSpec(memory_space=pltpu.SMEM)
VMEM = pl.BlockSpec(memory_space=pltpu.VMEM)


def small_params():
    return pltpu.CompilerParams(vmem_limit_bytes=20 * 2**20)


def small_cost(flops, size):
    return pl.CostEstimate(flops=flops, bytes_accessed=size, transcendentals=0)


def join_kernel(sizes, *refs):
    out, top = refs[-1], 0
    for ref, size in zip(refs, sizes):
        out[top : top + size] = ref[...]
        top += size


def join(*arrays):
    sizes = [a.shape[0] for a in arrays]
    shape = (sum(sizes), *arrays[0].shape[1:])
    return pl.pallas_call(
        functools.partial(join_kernel, sizes),
        out_shape=jax.ShapeDtypeStruct(shape, arrays[0].dtype),
        in_specs=[VMEM] * len(arrays),
        out_specs=VMEM,
        compiler_params=small_params(),
        cost_estimate=small_cost(0, 2**20),
        name="join",
    )(*arrays)


def down_kernel(core_ref, own_ref, other_ref, policy_ref, frozen_ref, out_ref):
    core = core_ref[0]

    def both(weight_ref):
        weight = weight_ref[...]
        for ref, place in ((own_ref, core), (other_ref, 1 - core)):
            raw = lax.dot_general(
                ref[...], weight, (((1,), (1,)), ((), ())), preferred_element_type=jnp.float32
            )
            out_ref[pl.ds(place * 4, 4)] = raw.reshape(4, PIECE, L + QR)

    @pl.when(core == 0)
    def _():
        both(policy_ref)

    @pl.when(core == 1)
    def _():
        both(frozen_ref)


def project_down(core, own, other, policy, frozen):
    return pl.pallas_call(
        down_kernel,
        out_shape=jax.ShapeDtypeStruct((8, PIECE, L + QR), jnp.float32),
        in_specs=[SMEM] + [VMEM] * 4,
        out_specs=VMEM,
        compiler_params=small_params(),
        cost_estimate=small_cost(2 * ROWS * 896 * 576, 3 * 2**20),
        name="project_down",
    )(core[None], own, other, policy, frozen)


def absorb_kernel(place_ref, policy_ref, frozen_ref, other_ref, *refs):
    shard_refs, (out_ref, value_ref, up_ref, own_ref) = refs[:8], refs[8:]
    core, z, yl = place_ref[0], place_ref[1], place_ref[2]
    own_ref[...] = jnp.where(core == 0, policy_ref[...], frozen_ref[...])
    for shift in range(8):
        top = lax.rem(z + shift, 8) * (L // 8)
        for part in range(4):
            from_yl = lax.rem(yl + part // 2, 2)
            from_core = lax.rem(core + part % 2, 2)
            start = top + (from_yl * 2 + from_core) * 16
            place = pl.ds(pl.multiple_of(start, 16), 16)
            for h in range(HEADS):
                up_ref[h, place, :] = shard_refs[shift][part, h]
    for h in range(HEADS):
        left = h * (QN + QR)
        for ref, half in ((own_ref, core), (other_ref, 1 - core)):
            here = pl.ds(pl.multiple_of(h * ROWS + half * BLOCK, BLOCK), BLOCK)
            absorbed = lax.dot_general(
                ref[:, left : left + QN],
                up_ref[h, :, :QN],
                (((1,), (1,)), ((), ())),
                preferred_element_type=jnp.float32,
            )
            out_ref[here, :L] = absorbed.astype(jnp.bfloat16)
            out_ref[here, L:] = ref[:, left + QN : left + QN + QR]
        value_ref[h] = up_ref[h, :, QN:]


def absorb(place, policy, frozen, other, shards_by_shift):
    return pl.pallas_call(
        absorb_kernel,
        out_shape=(
            jax.ShapeDtypeStruct((HEADS * ROWS, L + QR), jnp.bfloat16),
            jax.ShapeDtypeStruct((HEADS, L, VD), jnp.bfloat16),
        ),
        in_specs=[SMEM] + [VMEM] * 11,
        out_specs=(VMEM, VMEM),
        scratch_shapes=[
            pltpu.VMEM((HEADS, L, QN + VD), jnp.bfloat16),
            pltpu.VMEM((BLOCK, HEADS * (QN + QR)), jnp.bfloat16),
        ],
        compiler_params=small_params(),
        cost_estimate=small_cost(2 * HEADS * ROWS * QN * L, 9 * 2**20),
        name="absorb",
    )(place, policy, frozen, other, *shards_by_shift)


CALLS = ((0,), (1, 3), (2,))
TILES, OPENS, USED = 124, 125, 126


def pack(slot, kind_0, kind_1, begin):
    return slot | (kind_0 << 8) | (kind_1 << 10) | (begin << 12)


def plan_kernel(place_ref, own_ref, other_ref, out_ref, part_ref, kind_ref):
    core, z, yl, first, second = (place_ref[i] for i in range(5))
    is_first = core == 0

    def one_block(block, carry):
        own, other = own_ref[0, block], other_ref[0, block]
        kind_0, kind_1 = jnp.where(is_first, own, other), jnp.where(is_first, other, own)
        kind_ref[block] = pack(0, kind_0, kind_1, block * BLOCK)
        return carry

    lax.fori_loop(0, 32, one_block, 0)
    both_open = pack(0, 1, 1, 0)
    any_kind = pack(0, 3, 3, 0)
    counts = []
    for call, offsets in enumerate(CALLS):
        opens, partly = 0, 0
        for index, rb in enumerate(offsets):
            at_b = second ^ rb
            for ra in range(4):
                at_a = first ^ ra
                piece_y = jnp.where(is_first, at_a, at_b)
                piece_x = jnp.where(is_first, at_b, at_a)
                shift = (piece_y & 1) * 2 + (piece_y >> 1)
                extra = pack(index * SLOTS + ra * 8, 0, 0, piece_x * PIECE)
                for rz in range(8):
                    piece_z = lax.rem(z + (rz & 6), 8) ^ (rz & 1)
                    item = kind_ref[piece_z * 4 + shift] + (extra + rz)
                    kinds = item & any_kind
                    is_open = kinds == both_open
                    out_ref[call, opens] = item
                    part_ref[call, partly] = item
                    opens = opens + is_open.astype(jnp.int32)
                    partly = partly + (jnp.logical_not(is_open) & (kinds != 0)).astype(jnp.int32)
        counts.append((opens, partly))

    moved = 0
    for call, (opens, partly) in enumerate(counts):

        def append(i, carry, call=call, opens=opens):
            out_ref[call, opens + i] = part_ref[call, i]
            return carry

        lax.fori_loop(0, partly, append, 0)
        used = opens + partly
        if call:

            def take(i, carry, call=call, used=used, start=start):
                item = out_ref[call - 1, start + i]
                slot = len(CALLS[call]) * SLOTS + i
                out_ref[call, used + i] = (item & ~255) | slot
                return carry

            lax.fori_loop(0, moved, take, 0)
            used = used + moved
        tiles = lax.div(used + (PER_TILE - 1), PER_TILE)
        if call < len(CALLS) - 1:
            spare = lax.rem(used, PER_TILE)
            coming = counts[call + 1][0] + counts[call + 1][1]
            room = lax.rem(PER_TILE - lax.rem(coming, PER_TILE), PER_TILE)
            moved = jnp.where(spare <= room, spare, 0)
            out_ref[call, USED] = used
            used = used - moved
            tiles = lax.div(used + (PER_TILE - 1), PER_TILE)
            start = used

        def fill(i, carry, call=call):
            out_ref[call, i] = 0
            return carry

        if call < len(CALLS) - 1:
            lax.fori_loop(jnp.where(moved > 0, tiles * PER_TILE, used), tiles * PER_TILE, fill, 0)
        else:
            lax.fori_loop(used, tiles * PER_TILE, fill, 0)
        out_ref[call, TILES] = tiles
        out_ref[call, OPENS] = opens


def make_plan(place, own_kind, other_kind):
    return pl.pallas_call(
        plan_kernel,
        out_shape=jax.ShapeDtypeStruct((len(CALLS), 128), jnp.int32),
        in_specs=[SMEM] * 3,
        out_specs=SMEM,
        scratch_shapes=[pltpu.SMEM((3, 128), jnp.int32), pltpu.SMEM((32,), jnp.int32)],
        compiler_params=small_params(),
        cost_estimate=small_cost(0, 4096),
        name="plan",
    )(place, own_kind, other_kind)


def attend_kernel(call, chunks, first, final, *refs):
    refs = list(refs)
    plan_ref, place_ref, q_ref = refs[:3]
    key_refs = refs[3 : 3 + chunks]
    refs = refs[3 + chunks :]
    if not first:
        in_stat, in_acc = refs[:2]
        refs = refs[2:]
    if final:
        value_ref, keep_ref, send_ref = refs[:3]
        refs = refs[3:]
    else:
        left_ref, out_stat, out_acc = refs[:3]
        refs = refs[3:]
    acc, top, total, tile_ref, bias_ref, score_ref, other_ref = refs
    height, steps = GROUP * ROWS, HEADS // GROUP
    core, row_base = place_ref[0], (place_ref[1] * 2 + place_ref[2]) * ROWS
    tiles, opens = plan_ref[call, TILES], plan_ref[call, OPENS]
    half = SLOTS // 2

    def has_unseen(t):
        return (t + 1) * PER_TILE > opens

    def score(query, t):
        keys = tile_ref[pl.ds(pl.multiple_of(t * TILE, TILE), TILE), :]
        return lax.dot_general(
            query, keys, (((1,), (1,)), ((), ())), preferred_element_type=jnp.float32
        )

    def piece_at(index):
        slot = plan_ref[call, index] & 255
        inside = lax.rem(slot, half)
        piece = key_refs[0][inside]
        for i in range(1, chunks):
            piece = jnp.where(slot >= i * half, key_refs[i][inside], piece)
        return piece

    if not final:

        def leave(index, carry):
            left_ref[index - tiles * PER_TILE] = piece_at(index)
            return carry

        lax.fori_loop(tiles * PER_TILE, plan_ref[call, USED], leave, 0)

    def gather(t, carry):
        for s in range(PER_TILE):
            place = pl.ds(pl.multiple_of(t * TILE + s * PIECE, PIECE), PIECE)
            tile_ref[place, :] = piece_at(t * PER_TILE + s)

        @pl.when(has_unseen(t))
        def _():
            lane = lax.broadcasted_iota(jnp.int32, (1, TILE), 1)
            kind_0 = jnp.zeros_like(lane)
            kind_1, begin = kind_0, kind_0
            for s in range(PER_TILE):
                item = plan_ref[call, t * PER_TILE + s]
                here = lane // PIECE == s
                kind_0 = jnp.where(here, (item >> 8) & 3, kind_0)
                kind_1 = jnp.where(here, (item >> 10) & 3, kind_1)
                begin = jnp.where(here, item >> 12, begin)
            key_row = begin + lane % PIECE
            row = lax.broadcasted_iota(jnp.int32, (ROWS, TILE), 0)
            kind = jnp.where(row < BLOCK, kind_0, kind_1)
            seen = (kind == 1) | ((kind == 2) & (key_row <= row + row_base))
            bias_ref[t] = jnp.where(seen, 0.0, MASKED)

        return carry

    lax.fori_loop(0, tiles, gather, 0)

    @pl.when(tiles > 0)
    def _():
        score_ref[...] = score(q_ref[:height, :], 0)

    def start_step(step, carry):
        mine = pl.ds(pl.multiple_of(step * height, height), height)
        if first:
            top[mine, :] = jnp.full((height, 128), START, jnp.float32)
            total[mine, :] = jnp.zeros((height, 128), jnp.float32)
            acc[mine, :] = jnp.zeros((height, L), jnp.float32)
        else:
            top[mine, :] = jnp.broadcast_to(in_stat[mine, :1], (height, 128))
            total[mine, :] = jnp.broadcast_to(in_stat[mine, 64:65], (height, 128))
            acc[mine, :] = in_acc[mine, :]
        return carry

    lax.fori_loop(0, steps, start_step, 0)

    def one_tile(i, now_ref, next_ref):
        step = lax.div(i, tiles)
        t = i - step * tiles
        mine = pl.ds(pl.multiple_of(step * height, height), height)
        ahead = jnp.minimum(i + 1, steps * tiles - 1)
        next_step = lax.div(ahead, tiles)
        theirs = pl.ds(pl.multiple_of(next_step * height, height), height)

        @pl.when(has_unseen(t))
        def _():
            for g in range(GROUP):
                here = slice(g * ROWS, (g + 1) * ROWS)
                now_ref[here, :] = now_ref[here, :] + bias_ref[t]

        next_ref[...] = score(q_ref[theirs, :], ahead - next_step * tiles)
        scores = now_ref[...]
        old = top[mine, :]
        new = jnp.maximum(old, jnp.max(scores, axis=1, keepdims=True))
        exps = jnp.exp2((scores - new[:, :1]) * SCALE2)
        shrink = jnp.exp2((old - new) * SCALE2)
        top[mine, :] = new
        total[mine, :] = total[mine, :] * shrink + jnp.sum(exps, axis=1, keepdims=True)
        values = tile_ref[pl.ds(pl.multiple_of(t * TILE, TILE), TILE), :L]
        mixed = jnp.dot(exps.astype(jnp.bfloat16), values, preferred_element_type=jnp.float32)
        acc[mine, :] = acc[mine, :] * shrink[:, :1] + mixed

    def two_tiles(pair, carry):
        one_tile(2 * pair, score_ref, other_ref)
        one_tile(2 * pair + 1, other_ref, score_ref)
        return carry

    lax.fori_loop(0, steps // 2 * tiles, two_tiles, 0)

    def end_step(step, carry):
        mine = pl.ds(pl.multiple_of(step * height, height), height)
        if final:
            context = (acc[mine, :] * (1.0 / total[mine, :1])).astype(jnp.bfloat16)
            for g in range(GROUP):
                mixed = jnp.dot(
                    context[g * ROWS : (g + 1) * ROWS], value_ref[step * GROUP + g], preferred_element_type=jnp.float32
                ).astype(jnp.bfloat16)
                left, right = mixed[:BLOCK], mixed[BLOCK:]
                columns = pl.ds(pl.multiple_of((step * GROUP + g) * VD, VD), VD)
                keep_ref[:, columns] = jnp.where(core == 0, left, right)
                send_ref[:, columns] = jnp.where(core == 0, right, left)
        else:
            lane = lax.broadcasted_iota(jnp.int32, (height, 128), 1)
            out_stat[mine, :] = jnp.where(lane < 64, top[mine, :], total[mine, :])
            out_acc[mine, :] = acc[mine, :]
        return carry

    lax.fori_loop(0, steps, end_step, 0)


def attend(call, plan, place, query, keys, carry, value):
    chunks = len(keys)
    first, final = carry is None, value is not None
    most = (chunks * SLOTS // 2 + PER_TILE - 1) // PER_TILE
    height = GROUP * ROWS
    operands = [plan, place, query, *keys]
    specs = [SMEM] * 2 + [VMEM] * (1 + chunks)
    if not first:
        operands += list(carry)
        specs += [VMEM] * 2
    scratch = [
        pltpu.VMEM((HEADS * ROWS, L), jnp.float32),
        pltpu.VMEM((HEADS * ROWS, 128), jnp.float32),
        pltpu.VMEM((HEADS * ROWS, 128), jnp.float32),
        pltpu.VMEM((most * TILE, L + QR), jnp.bfloat16),
        pltpu.VMEM((most, ROWS, TILE), jnp.float32),
        pltpu.VMEM((height, TILE), jnp.float32),
        pltpu.VMEM((height, TILE), jnp.float32),
    ]
    if final:
        operands.append(value)
        specs.append(VMEM)
        one = jax.ShapeDtypeStruct((BLOCK, HEADS * VD), jnp.bfloat16)
        out_shape = (one, one)
        out_specs = (VMEM,) * 2
    else:
        left = jax.ShapeDtypeStruct((PER_TILE, PIECE, L + QR), jnp.bfloat16)
        out_shape = (
            left,
            jax.ShapeDtypeStruct((HEADS * ROWS, 128), jnp.float32),
            jax.ShapeDtypeStruct((HEADS * ROWS, L), jnp.float32),
        )
        out_specs = (VMEM,) * 3
    return pl.pallas_call(
        functools.partial(attend_kernel, call, chunks, first, final),
        out_shape=out_shape,
        in_specs=specs,
        out_specs=out_specs,
        scratch_shapes=scratch,
        compiler_params=pltpu.CompilerParams(vmem_limit_bytes=28 * 2**20),
        cost_estimate=pl.CostEstimate(
            flops=chunks * HEADS * ROWS * 1024 * 1280,
            bytes_accessed=chunks * 2**20 + 8 * 2**20,
            transcendentals=chunks * HEADS * ROWS * 512,
        ),
        name="attend",
    )(*operands)


def shards(
    hidden,
    block_kind,
    policy_queries,
    policy_down,
    policy_gain,
    policy_up,
    frozen_queries,
    frozen_down,
    frozen_gain,
    frozen_up,
):
    core = lax.axis_index("c")
    z = lax.axis_index("z")
    yl = lax.axis_index("yl")
    yh = lax.axis_index("yh")
    x = lax.axis_index("x")
    y = yh * 2 + yl
    is_policy = core == 0

    def mine(policy, frozen):
        return jnp.where(is_policy, policy, frozen)

    first_place, second_place = mine(y, x), mine(x, y)
    place = jnp.stack([core, z, yl, first_place, second_place])

    other_hidden = send(hidden, SWAP_CORE)
    own_up = mine(policy_up, frozen_up)
    other_up = send(mine(frozen_up, policy_up), SWAP_CORE)
    other_kind = send(block_kind, SWAP_CORE)
    raw = project_down(core, hidden, other_hidden, policy_down.T, frozen_down.T)
    raw, policy_queries, frozen_queries, other_kind, other_up = lax.optimization_barrier(
        (raw, policy_queries, frozen_queries, other_kind, other_up)
    )
    parts = lax.all_to_all(raw, FSDP, 0, 0)

    plan = make_plan(place, block_kind, other_kind)

    up_two = jnp.stack([own_up, other_up])
    up_here = jnp.concatenate([up_two, send(up_two, SWAP_YL)], axis=0)
    below, above = [up_here], [up_here]
    below.append(send(up_here, z_ring(1)))
    above.append(send(up_here, z_ring(-1)))
    parts, plan, below[1], above[1] = lax.optimization_barrier((parts, plan, below[1], above[1]))

    raw_sum = jnp.sum(parts, axis=0)
    first_row = (z * 2 + yl) * ROWS + (yh * 4 + x) * PIECE
    positions = (first_row + jnp.arange(PIECE, dtype=jnp.int32)).astype(jnp.float32)
    own_keys = finish_keys(raw_sum, mine(policy_gain, frozen_gain), positions)

    pair = jnp.stack([own_keys, send(own_keys, z_xor(1))])
    pair, below[1], above[1] = lax.optimization_barrier((pair, below[1], above[1]))
    for step in (1, 2):
        below.append(send(below[step], z_ring(1)))
        above.append(send(above[step], z_ring(-1)))
    opposite = send(below[3], z_ring(1))
    by_shift = [up_here, above[1], above[2], above[3], opposite, below[3], below[2], below[1]]

    other_queries = send(mine(frozen_queries, policy_queries), SWAP_CORE)
    query, value = absorb(place, policy_queries, frozen_queries, other_queries, by_shift)

    pair_below, pair_above = send(pair, z_ring(2)), send(pair, z_ring(-2))
    pair_far = send(pair, z_ring(4))
    held = join(pair, pair_above, pair_far, pair_below)
    near1 = send(held, first_axis(1))
    near3 = send(held, first_axis(3))
    far = send(held, first_axis(2))
    low = join(held, near1)
    side3_low = send(low, second_axis(3))
    side1_low = send(low, second_axis(1))
    high = join(far, near3)
    side1_high = send(high, second_axis(1))
    side3_high = send(high, second_axis(3))
    left, *carry = attend(0, plan, place, query, [low, high], None, None)
    side2_low = send(side3_low, second_axis(1))
    side2_high = send(side1_high, second_axis(3))
    sides = [side1_low, side1_high, side3_low, side3_high]
    left, *carry = attend(1, plan, place, query, [*sides, left], carry, None)
    kept, sent = attend(2, plan, place, query, [side2_low, side2_high, left], carry, value)

    got = send(sent, SWAP_CORE)
    return jnp.where(is_policy, kept, got), jnp.where(is_policy, got, kept)


def solution(mesh):
    fine = Mesh(mesh.devices.reshape(SIZES), NAMES)
    return jax.shard_map(
        shards,
        mesh=fine,
        in_specs=(
            P(CTX, FSDP),
            P(CTX, None),
            P(CTX, FSDP),
            P(FSDP, None),
            P(),
            P(FSDP, CTX, None),
            P(CTX, FSDP),
            P(FSDP, None),
            P(),
            P(FSDP, CTX, None),
        ),
        out_specs=(P(CTX, FSDP), P(CTX, FSDP)),
        check_vma=False,
    )
```
